256 devices in a mesh: task: 2 (over x_lo), dp: 16 (over z, core), mp: 8 (over x_hi, y).
Axes of the slice: x: 4 (x_hi: 2, x_lo: 2; x = x_hi * 2 + x_lo), y: 4, z: 8, core: 2. Of those that a mesh axis runs over, the one named last changes fastest.
Arguments:
- deltas: bfloat16 [6, 4096, 4608], P('task', 'dp', 'mp'), may hold values from -400 to 400, as said below
- fishers: bfloat16 [6, 4096, 4608], P('task', 'dp', 'mp'), may hold values from 0.0009994507 to 1
Outputs:
- merged_out: float32 [4096, 4608], P('dp', 'mp')
The draws below stay inside these ranges and needn't reach their ends.
Inputs may be any that keep to these rules, and one draw needn't show every extreme that they name: `deltas`: Real-valued weight differences.
All inputs are finite; a program needn't handle non-finite values.
Results may differ from the reference program's by a relative error of at most 0.0003.
Values sent between devices are 32-bit elements; how exact they have to be, the bound alone decides.
No kernel may reach another device: no remote copies, remote signals or barrier semaphores. Data moves between devices by JAX's collectives and lax.ppermute only.
A program may use at most 64 MiB of HBM per device.

```python
import math
import jax
import jax.numpy as jnp
from jax import lax

D = 4608
ROW_DEV = 256
ROWS = 4096
TASKS = 6


def draw_deltas(key, part):
    keys = jax.random.split(jax.random.fold_in(key, 11), 5)
    row_index = jnp.arange(ROWS, dtype=jnp.int32)
    row_pos = row_index.astype(jnp.float32) / ROWS
    inner_pos = (row_index % ROW_DEV).astype(jnp.float32) / ROW_DEV
    col_pos = jnp.arange(D, dtype=jnp.float32) / D
    noise = jnp.clip(jax.random.normal(keys[0], (TASKS, ROWS, D), jnp.float32), -6.0, 6.0)
    row_rise = 3.0 ** (row_pos - 0.5) * 3.0 ** (inner_pos - 0.5)
    row_scale = jnp.exp(jax.random.uniform(keys[2], (ROWS,), jnp.float32, 0.0, math.log(10.0))) / 4.6 * row_rise
    col_scale = jnp.exp(jax.random.uniform(keys[3], (D,), jnp.float32, 0.0, math.log(10.0))) / 4.6 * 3.0 ** (col_pos - 0.5)
    task_scale = jnp.exp(jax.random.uniform(keys[4], (TASKS,), jnp.float32, -0.7, 0.7))
    values = noise * row_scale[None, :, None] * col_scale[None, None, :] * task_scale[:, None, None]
    return values.astype(jnp.bfloat16)


def shard_levels(own_key, shape, pieces, least, top_value):
    level, own = 1.0, jax.random.fold_in(own_key, 6)
    for dim, parts in pieces:
        draws = jnp.exp(jax.random.uniform(jax.random.fold_in(own, dim), (parts,), jnp.float32, least / len(pieces), top_value / len(pieces)))
        level = level * jnp.repeat(draws, shape[dim] // parts).reshape([-1 if axis == dim else 1 for axis in range(len(shape))])
    return level


def setup_inputs(seed: int = 0) -> dict:
    seeds = jax.random.split(jax.random.key(seed), 3)
    return {
        "deltas": draw_deltas(jax.random.fold_in(seeds[2], 71), 0),
        "fishers": jnp.clip(jnp.exp(math.log(1.0) - 6.9083047 * jax.random.uniform(seeds[1], (TASKS, ROWS, D), jnp.float32) ** shard_levels(seeds[1], (TASKS, ROWS, D), ((0, 2), (1, 16), (2, 8)), -0.2, 0.2)), 0.0009994507, 1.0).astype(jnp.bfloat16),
    }


def reference(deltas, fishers):
    weights = fishers.astype(jnp.float32)
    widened = deltas.astype(jnp.float32)
    numerator = lax.optimization_barrier(jnp.sum(weights * widened, axis=0))
    denominator = lax.optimization_barrier(jnp.sum(weights, axis=0))
    merged = numerator / denominator
    task_sq = lax.optimization_barrier(jnp.sum(widened * widened, axis=(1, 2)))
    merged_sq = jnp.sum(merged * merged)
    rescale = jnp.mean(jnp.sqrt(task_sq + 1e-06)) / jnp.sqrt(merged_sq + 1e-06)
    return rescale * merged
```

```python
import jax
import jax.numpy as jnp
from jax import lax
from jax.sharding import PartitionSpec as P

AXES = ("task", "dp", "mp")
SWAP = [(0, 1), (1, 0)]
EPS = 1e-06


def weighted_sums(deltas, fishers, start, size):
    d = lax.dynamic_slice_in_dim(deltas, start, size, 1).astype(jnp.float32)
    f = lax.dynamic_slice_in_dim(fishers, start, size, 1).astype(jnp.float32)
    return jnp.stack([jnp.sum(f * d, axis=0), jnp.sum(f, axis=0)])


def from_everyone(values, axes):
    size = lax.axis_size(axes)
    return lax.all_to_all(jnp.broadcast_to(values[None], (size, *values.shape)), axes, 0, 0, tiled=True)


def shards(deltas, fishers):
    deltas, fishers = jnp.swapaxes(deltas, 1, 2), jnp.swapaxes(fishers, 1, 2)
    held, columns, _ = deltas.shape
    half = columns // 2
    task = lax.axis_index("task")
    sent = weighted_sums(deltas, fishers, (1 - task) * half, half)
    received = lax.ppermute(sent, "task", SWAP)
    own = weighted_sums(deltas, fishers, task * half, half)
    wide = deltas.astype(jnp.float32)
    task_sums = jnp.sum(wide * wide, axis=(1, 2))
    total = own + received
    merged = total[0] / total[1]
    merged_sum = jnp.sum(merged * merged)
    other = lax.ppermute(merged, "task", SWAP)
    sums = from_everyone(jnp.concatenate([task_sums, merged_sum[None]]), AXES)
    sums = jnp.sum(sums.reshape(2, -1, held + 1), axis=1)
    target = jnp.mean(jnp.sqrt(sums[:, :held] + EPS))
    rescale = target / jnp.sqrt(jnp.sum(sums[:, held]) + EPS)
    low = jnp.where(task == 0, merged, other)
    high = jnp.where(task == 0, other, merged)
    return (rescale * jnp.concatenate([low, high])).T


def solution(mesh):
    placed = P("task", "dp", "mp")
    return jax.shard_map(shards, mesh=mesh, in_specs=(placed, placed), out_specs=P("dp", "mp"), check_vma=False)
```

```python
import functools

import jax
import jax.numpy as jnp
from jax import lax
from jax.experimental import pallas as pl
from jax.experimental.pallas import tpu as pltpu
from jax.sharding import PartitionSpec as P

AXES = ("task", "dp", "mp")
SWAP = [(0, 1), (1, 0)]
EPS = 1e-06
LANES = 128
PIECES = 3
SMALL = pltpu.CompilerParams(vmem_limit_bytes=16 * 1024 * 1024)


def whole():
    return pl.BlockSpec(memory_space=pltpu.VMEM)


def hbm():
    return pl.BlockSpec(memory_space=pltpu.HBM)


def fetches(d_hbm, f_hbm, d_ref, f_ref, sems, start, at, size):
    pairs = []
    for k in range(d_hbm.shape[0]):
        pairs.append(tuple(
            pltpu.make_async_copy(src.at[k, pl.ds(start, size), :], dst.at[k, pl.ds(at, size), :], sems.at[2 * k + i])
            for i, (src, dst) in enumerate(((d_hbm, d_ref), (f_hbm, f_ref)))
        ))
    return pairs


def add_weighted(pairs, d_ref, f_ref, sums_ref):
    _, rows, _ = sums_ref.shape
    for k, pair in enumerate(pairs):
        for copy in pair:
            copy.wait()
        d = d_ref[k, :rows, :].astype(jnp.float32)
        f = f_ref[k, :rows, :].astype(jnp.float32)
        if k == 0:
            sums_ref[0], sums_ref[1] = f * d, f
        else:
            sums_ref[0] += f * d
            sums_ref[1] += f


def send_kernel(d_hbm, f_hbm, sums_ref, d_ref, f_ref, sems):
    _, rows, _ = sums_ref.shape
    start = pl.multiple_of((1 - lax.axis_index("task")) * rows, 32)
    pairs = fetches(d_hbm, f_hbm, d_ref, f_ref, sems, start, 0, rows)
    for pair in pairs:
        for copy in pair:
            copy.start()
    add_weighted(pairs, d_ref, f_ref, sums_ref)


def own_kernel(d_hbm, f_hbm, sums_ref, squares_ref, d_ref, f_ref, sems, rest_sems):
    _, rows, _ = sums_ref.shape
    held, both, columns = d_hbm.shape
    task = lax.axis_index("task")
    pairs = fetches(d_hbm, f_hbm, d_ref, f_ref, sems, pl.multiple_of(task * rows, 32), 0, rows)
    for pair in pairs:
        for copy in pair:
            copy.start()
    start = pl.multiple_of((1 - task) * rows, 32)
    rest = [
        pltpu.make_async_copy(
            d_hbm.at[k, pl.ds(start, rows), :], d_ref.at[k, pl.ds(rows, rows), :], rest_sems.at[k]
        )
        for k in range(held)
    ]
    for copy in rest:
        copy.start()
    add_weighted(pairs, d_ref, f_ref, sums_ref)
    for k in range(held):
        rest[k].wait()
        d = d_ref[k].astype(jnp.float32)
        part = jnp.sum((d * d).reshape(both // 8, 8, columns), axis=0)
        squares_ref[k] = part[:, :LANES] + part[:, LANES:]


def merge_kernel(own_ref, got_ref, squares_ref, merged_ref, message_ref):
    _, rows, columns = own_ref.shape
    merged = (own_ref[0] + got_ref[0]) / (own_ref[1] + got_ref[1])
    merged_ref[...] = merged
    part = jnp.sum((merged * merged).reshape(rows // 8, 8, columns), axis=0)
    merged_sum = jnp.sum(part, keepdims=True)
    held = squares_ref.shape[0]
    lane = lax.broadcasted_iota(jnp.int32, (1, LANES), 1)
    first = lax.axis_index("task") * held
    message = jnp.where(lane == 2 * held, merged_sum, 0.0)
    for k in range(held):
        message = jnp.where(lane == first + k, jnp.sum(squares_ref[k], keepdims=True), message)
    message_ref[...] = jnp.broadcast_to(message, message_ref.shape)


def scale_kernel(tasks, messages_ref, merged_ref, other_ref, out_hbm, scaled_ref, sems):
    rows, _ = merged_ref.shape
    sums = jnp.sum(messages_ref[...], axis=0, keepdims=True)
    lane = lax.broadcasted_iota(jnp.int32, sums.shape, 1)
    target = jnp.sum(jnp.where(lane < tasks, jnp.sqrt(sums + EPS), 0.0), keepdims=True) / tasks
    merged_sq = jnp.sum(jnp.where(lane == tasks, sums, 0.0), keepdims=True)
    rescale = target / jnp.sqrt(merged_sq + EPS)
    task = lax.axis_index("task")
    size = rows // PIECES
    copies = []
    for i, (half_ref, side) in enumerate(((merged_ref, task), (other_ref, 1 - task))):
        for j in range(PIECES):
            at = (i * PIECES + j) * size
            scaled_ref[at : at + size, :] = rescale * half_ref[j * size : (j + 1) * size, :]
            to = pl.multiple_of(side * rows + j * size, 8)
            copies.append(pltpu.make_async_copy(
                scaled_ref.at[at : at + size, :], out_hbm.at[pl.ds(to, size), :], sems.at[i * PIECES + j]
            ))
            copies[-1].start()
    for copy in copies:
        copy.wait()


def shards(deltas, fishers):
    deltas, fishers = jnp.swapaxes(deltas, 1, 2), jnp.swapaxes(fishers, 1, 2)
    deltas = pltpu.with_memory_space_constraint(deltas, pltpu.HBM)
    fishers = pltpu.with_memory_space_constraint(fishers, pltpu.HBM)
    held, columns, rows = deltas.shape
    half = columns // 2
    tasks, devices = held * lax.axis_size("task"), lax.axis_size(AXES)
    sums_type = jax.ShapeDtypeStruct((2, half, rows), jnp.float32)
    half_type = jax.ShapeDtypeStruct((half, rows), jnp.float32)
    half_input = pltpu.VMEM((held, half, rows), deltas.dtype)
    sent = pl.pallas_call(
        send_kernel, out_shape=sums_type, in_specs=[hbm()] * 2, out_specs=whole(), compiler_params=SMALL,
        scratch_shapes=[half_input, half_input, pltpu.SemaphoreType.DMA((2 * held,))],
    )(deltas, fishers)
    received = lax.ppermute(sent, "task", SWAP)
    own, squares = pl.pallas_call(
        own_kernel, out_shape=(sums_type, jax.ShapeDtypeStruct((held, 8, LANES), jnp.float32)),
        in_specs=[hbm()] * 2, out_specs=(whole(), whole()), compiler_params=SMALL,
        scratch_shapes=[
            pltpu.VMEM((held, columns, rows), deltas.dtype), half_input,
            pltpu.SemaphoreType.DMA((2 * held,)), pltpu.SemaphoreType.DMA((held,)),
        ],
    )(deltas, fishers)
    merged, message = pl.pallas_call(
        merge_kernel, out_shape=(half_type, jax.ShapeDtypeStruct((devices, LANES), jnp.float32)),
        in_specs=[whole()] * 3, out_specs=(whole(), whole()), compiler_params=SMALL,
    )(own, received, squares)
    other = lax.ppermute(merged, "task", SWAP)
    messages = lax.all_to_all(message, AXES, 0, 0, tiled=True)
    out = pl.pallas_call(
        functools.partial(scale_kernel, tasks), out_shape=jax.ShapeDtypeStruct((columns, rows), jnp.float32),
        in_specs=[whole()] * 3, out_specs=hbm(), compiler_params=SMALL,
        scratch_shapes=[pltpu.VMEM((columns, rows), jnp.float32), pltpu.SemaphoreType.DMA((2 * PIECES,))],
    )(messages, merged, other)
    return out.T


def solution(mesh):
    placed = P("task", "dp", "mp")
    return jax.shard_map(shards, mesh=mesh, in_specs=(placed, placed), out_specs=P("dp", "mp"), check_vma=False)
```

```python
import functools

import jax
import jax.numpy as jnp
from jax import lax
from jax.experimental import pallas as pl
from jax.experimental.pallas import tpu as pltpu
from jax.sharding import PartitionSpec as P

AXES = ("task", "dp", "mp")
SWAP = [(0, 1), (1, 0)]
EPS = 1e-06
LANES = 128
PIECES = 3
FIRST = (2, 2, 4)
SMALL = pltpu.CompilerParams(vmem_limit_bytes=16 * 1024 * 1024)


def whole():
    return pl.BlockSpec(memory_space=pltpu.VMEM)


def hbm():
    return pl.BlockSpec(memory_space=pltpu.HBM)


def fetches(d_hbm, f_hbm, d_ref, f_ref, sems, start, at, size):
    pairs = []
    for k in range(d_hbm.shape[0]):
        pairs.append(tuple(
            pltpu.make_async_copy(src.at[k, pl.ds(start, size), :], dst.at[k, pl.ds(at, size), :], sems.at[2 * k + i])
            for i, (src, dst) in enumerate(((d_hbm, d_ref), (f_hbm, f_ref)))
        ))
    return pairs


def add_weighted(pairs, d_ref, f_ref, sums_ref):
    _, rows, _ = sums_ref.shape
    for k, pair in enumerate(pairs):
        for copy in pair:
            copy.wait()
        d = d_ref[k, :rows, :].astype(jnp.float32)
        f = f_ref[k, :rows, :].astype(jnp.float32)
        if k == 0:
            sums_ref[0], sums_ref[1] = f * d, f
        else:
            sums_ref[0] += f * d
            sums_ref[1] += f


def send_kernel(d_hbm, f_hbm, sums_ref, d_ref, f_ref, sems):
    _, rows, _ = sums_ref.shape
    start = pl.multiple_of((1 - lax.axis_index("task")) * rows, 32)
    pairs = fetches(d_hbm, f_hbm, d_ref, f_ref, sems, start, 0, rows)
    for pair in pairs:
        for copy in pair:
            copy.start()
    add_weighted(pairs, d_ref, f_ref, sums_ref)


def own_kernel(d_hbm, f_hbm, sums_ref, squares_ref, d_ref, f_ref, sems, rest_sems):
    _, rows, _ = sums_ref.shape
    held, both, columns = d_hbm.shape
    task = lax.axis_index("task")
    pairs = fetches(d_hbm, f_hbm, d_ref, f_ref, sems, pl.multiple_of(task * rows, 32), 0, rows)
    for pair in pairs:
        for copy in pair:
            copy.start()
    start = pl.multiple_of((1 - task) * rows, 32)
    rest = [
        pltpu.make_async_copy(
            d_hbm.at[k, pl.ds(start, rows), :], d_ref.at[k, pl.ds(rows, rows), :], rest_sems.at[k]
        )
        for k in range(held)
    ]
    for copy in rest:
        copy.start()
    add_weighted(pairs, d_ref, f_ref, sums_ref)
    for k in range(held):
        rest[k].wait()
        d = d_ref[k].astype(jnp.float32)
        part = jnp.sum((d * d).reshape(both // 8, 8, columns), axis=0)
        squares_ref[k] = part[:, :LANES] + part[:, LANES:]


def merge_kernel(own_ref, got_ref, squares_ref, merged_ref, message_ref):
    _, rows, columns = own_ref.shape
    merged = (own_ref[0] + got_ref[0]) / (own_ref[1] + got_ref[1])
    merged_ref[...] = merged
    part = jnp.sum((merged * merged).reshape(rows // 8, 8, columns), axis=0)
    merged_sum = jnp.sum(part, keepdims=True)
    held = squares_ref.shape[0]
    lane = lax.broadcasted_iota(jnp.int32, (1, LANES), 1)
    first = lax.axis_index("task") * held
    message = jnp.where(lane == 2 * held, merged_sum, 0.0)
    for k in range(held):
        message = jnp.where(lane == first + k, jnp.sum(squares_ref[k], keepdims=True), message)
    message_ref[...] = message


def scale_kernel(tasks, messages_ref, merged_ref, other_ref, out_hbm, scaled_ref, sems):
    rows, _ = merged_ref.shape
    sums = jnp.sum(messages_ref[...], axis=0, keepdims=True)
    lane = lax.broadcasted_iota(jnp.int32, sums.shape, 1)
    target = jnp.sum(jnp.where(lane < tasks, jnp.sqrt(sums + EPS), 0.0), keepdims=True) / tasks
    merged_sq = jnp.sum(jnp.where(lane == tasks, sums, 0.0), keepdims=True)
    rescale = target / jnp.sqrt(merged_sq + EPS)
    task = lax.axis_index("task")
    size = rows // PIECES
    copies = []
    for i, (half_ref, side) in enumerate(((merged_ref, task), (other_ref, 1 - task))):
        for j in range(PIECES):
            at = (i * PIECES + j) * size
            scaled_ref[at : at + size, :] = rescale * half_ref[j * size : (j + 1) * size, :]
            to = pl.multiple_of(side * rows + j * size, 8)
            copies.append(pltpu.make_async_copy(
                scaled_ref.at[at : at + size, :], out_hbm.at[pl.ds(to, size), :], sems.at[i * PIECES + j]
            ))
            copies[-1].start()
    for copy in copies:
        copy.wait()


def groups_by_core(root):
    groups = []
    for core in range(2):
        places = []
        for task in range(2):
            for z in range(8):
                for x_hi in range(2):
                    for y in range(4):
                        place = (2 * x_hi + task, y, z)
                        index = ((task * 8 + z) * 2 + core) * 8 + x_hi * 4 + y
                        places.append((place != root, index))
        groups.append([index for _, index in sorted(places)])
    return groups


def shards(deltas, fishers):
    deltas, fishers = jnp.swapaxes(deltas, 1, 2), jnp.swapaxes(fishers, 1, 2)
    deltas = pltpu.with_memory_space_constraint(deltas, pltpu.HBM)
    fishers = pltpu.with_memory_space_constraint(fishers, pltpu.HBM)
    held, columns, rows = deltas.shape
    half = columns // 2
    tasks, devices = held * lax.axis_size("task"), lax.axis_size(AXES)
    sums_type = jax.ShapeDtypeStruct((2, half, rows), jnp.float32)
    half_type = jax.ShapeDtypeStruct((half, rows), jnp.float32)
    half_input = pltpu.VMEM((held, half, rows), deltas.dtype)
    sent = pl.pallas_call(
        send_kernel, out_shape=sums_type, in_specs=[hbm()] * 2, out_specs=whole(), compiler_params=SMALL,
        scratch_shapes=[half_input, half_input, pltpu.SemaphoreType.DMA((2 * held,))],
    )(deltas, fishers)
    received = lax.ppermute(sent, "task", SWAP)
    own, squares = pl.pallas_call(
        own_kernel, out_shape=(sums_type, jax.ShapeDtypeStruct((held, 8, LANES), jnp.float32)),
        in_specs=[hbm()] * 2, out_specs=(whole(), whole()), compiler_params=SMALL,
        scratch_shapes=[
            pltpu.VMEM((held, columns, rows), deltas.dtype), half_input,
            pltpu.SemaphoreType.DMA((2 * held,)), pltpu.SemaphoreType.DMA((held,)),
        ],
    )(deltas, fishers)
    merged, message = pl.pallas_call(
        merge_kernel, out_shape=(half_type, jax.ShapeDtypeStruct((1, LANES), jnp.float32)),
        in_specs=[whole()] * 3, out_specs=(whole(), whole()), compiler_params=SMALL,
    )(own, received, squares)
    other = lax.ppermute(merged, "task", SWAP)
    message += lax.ppermute(message, "dp", [(i, i ^ 1) for i in range(lax.axis_size("dp"))])
    messages = lax.all_to_all(
        jnp.broadcast_to(message, (devices // 2, LANES)), AXES, 0, 0, tiled=True, axis_index_groups=groups_by_core(FIRST)
    )
    out = pl.pallas_call(
        functools.partial(scale_kernel, tasks), out_shape=jax.ShapeDtypeStruct((columns, rows), jnp.float32),
        in_specs=[whole()] * 3, out_specs=hbm(), compiler_params=SMALL,
        scratch_shapes=[pltpu.VMEM((columns, rows), jnp.float32), pltpu.SemaphoreType.DMA((2 * PIECES,))],
    )(messages, merged, other)
    return out.T


def solution(mesh):
    placed = P("task", "dp", "mp")
    return jax.shard_map(shards, mesh=mesh, in_specs=(placed, placed), out_specs=P("dp", "mp"), check_vma=False)
```

```python
import functools

import jax
import jax.numpy as jnp
from jax import lax
from jax.experimental import pallas as pl
from jax.experimental.pallas import tpu as pltpu
from jax.sharding import PartitionSpec as P

AXES = ("task", "dp", "mp")
SWAP = [(0, 1), (1, 0)]
EPS = 1e-06
LANES = 128
EARLY = 64
PIECES = 3
FIRST = (2, 2, 5)
SMALL = pltpu.CompilerParams(vmem_limit_bytes=16 * 1024 * 1024)


def whole():
    return pl.BlockSpec(memory_space=pltpu.VMEM)


def hbm():
    return pl.BlockSpec(memory_space=pltpu.HBM)


def fetches(d_hbm, f_hbm, d_ref, f_ref, sems, start, at, size):
    pairs = []
    for k in range(d_hbm.shape[0]):
        pairs.append(tuple(
            pltpu.make_async_copy(src.at[k, pl.ds(start, size), :], dst.at[k, pl.ds(at, size), :], sems.at[2 * k + i])
            for i, (src, dst) in enumerate(((d_hbm, d_ref), (f_hbm, f_ref)))
        ))
    return pairs


def add_weighted(pairs, d_ref, f_ref, sums_ref):
    _, rows, _ = sums_ref.shape
    for k, pair in enumerate(pairs):
        for copy in pair:
            copy.wait()
        d = d_ref[k, :rows, :].astype(jnp.float32)
        f = f_ref[k, :rows, :].astype(jnp.float32)
        if k == 0:
            sums_ref[0], sums_ref[1] = f * d, f
        else:
            sums_ref[0] += f * d
            sums_ref[1] += f


def send_kernel(skip, d_hbm, f_hbm, sums_ref, d_ref, f_ref, sems):
    _, rows, _ = sums_ref.shape
    half = d_hbm.shape[1] // 2
    start = pl.multiple_of((1 - lax.axis_index("task")) * half + skip, 32)
    copies = [
        pltpu.make_async_copy(src.at[:, pl.ds(start, rows), :], dst, sems.at[i])
        for i, (src, dst) in enumerate(((d_hbm, d_ref), (f_hbm, f_ref)))
    ]
    for copy in copies:
        copy.start()
    for copy in copies:
        copy.wait()

    @pl.loop(0, rows // 32)
    def _(i):
        at = pl.ds(pl.multiple_of(i * 32, 32), 32)
        d = d_ref[:, at, :].astype(jnp.float32)
        f = f_ref[:, at, :].astype(jnp.float32)
        sums_ref[0, at, :] = jnp.sum(f * d, axis=0)
        sums_ref[1, at, :] = jnp.sum(f, axis=0)


def own_kernel(d_hbm, f_hbm, sums_ref, squares_ref, d_ref, f_ref, sems, rest_sems):
    _, rows, _ = sums_ref.shape
    held, both, columns = d_hbm.shape
    task = lax.axis_index("task")
    pairs = fetches(d_hbm, f_hbm, d_ref, f_ref, sems, pl.multiple_of(task * rows, 32), 0, rows)
    for pair in pairs:
        for copy in pair:
            copy.start()
    start = pl.multiple_of((1 - task) * rows, 32)
    rest = [
        pltpu.make_async_copy(
            d_hbm.at[k, pl.ds(start, rows), :], d_ref.at[k, pl.ds(rows, rows), :], rest_sems.at[k]
        )
        for k in range(held)
    ]
    for copy in rest:
        copy.start()
    add_weighted(pairs, d_ref, f_ref, sums_ref)
    for k in range(held):
        rest[k].wait()
        d = d_ref[k].astype(jnp.float32)
        part = jnp.sum((d * d).reshape(both // 8, 8, columns), axis=0)
        squares_ref[k] = part[:, :LANES] + part[:, LANES:]


def merge_kernel(own_ref, first_ref, rest_ref, squares_ref, merged_ref, message_ref):
    columns = own_ref.shape[2]
    at, part = 0, 0.0
    for got_ref in (first_ref, rest_ref):
        rows = got_ref.shape[1]
        own = own_ref[:, at : at + rows, :]
        merged = (own[0] + got_ref[0]) / (own[1] + got_ref[1])
        merged_ref[at : at + rows, :] = merged
        part += jnp.sum((merged * merged).reshape(rows // 8, 8, columns), axis=0)
        at += rows
    merged_sum = jnp.sum(part, keepdims=True)
    held = squares_ref.shape[0]
    lane = lax.broadcasted_iota(jnp.int32, (1, LANES), 1)
    first = lax.axis_index("task") * held
    message = jnp.where(lane == 2 * held, merged_sum, 0.0)
    for k in range(held):
        message = jnp.where(lane == first + k, jnp.sum(squares_ref[k], keepdims=True), message)
    message_ref[...] = message


def scale_kernel(tasks, messages_ref, merged_ref, other_ref, out_hbm, scaled_ref, sems):
    rows, _ = merged_ref.shape
    sums = jnp.sum(messages_ref[...], axis=0, keepdims=True)
    lane = lax.broadcasted_iota(jnp.int32, sums.shape, 1)
    target = jnp.sum(jnp.where(lane < tasks, jnp.sqrt(sums + EPS), 0.0), keepdims=True) / tasks
    merged_sq = jnp.sum(jnp.where(lane == tasks, sums, 0.0), keepdims=True)
    rescale = target / jnp.sqrt(merged_sq + EPS)
    task = lax.axis_index("task")
    size = rows // PIECES
    copies = []
    for i, (half_ref, side) in enumerate(((merged_ref, task), (other_ref, 1 - task))):
        for j in range(PIECES):
            at = (i * PIECES + j) * size
            scaled_ref[at : at + size, :] = rescale * half_ref[j * size : (j + 1) * size, :]
            to = pl.multiple_of(side * rows + j * size, 8)
            copies.append(pltpu.make_async_copy(
                scaled_ref.at[at : at + size, :], out_hbm.at[pl.ds(to, size), :], sems.at[i * PIECES + j]
            ))
            copies[-1].start()
    for copy in copies:
        copy.wait()


def groups_by_core(root):
    groups = []
    for core in range(2):
        places = []
        for task in range(2):
            for z in range(8):
                for x_hi in range(2):
                    for y in range(4):
                        place = (2 * x_hi + task, y, z)
                        index = ((task * 8 + z) * 2 + core) * 8 + x_hi * 4 + y
                        places.append((place != root, index))
        groups.append([index for _, index in sorted(places)])
    return groups


def shards(deltas, fishers):
    deltas, fishers = jnp.swapaxes(deltas, 1, 2), jnp.swapaxes(fishers, 1, 2)
    deltas = pltpu.with_memory_space_constraint(deltas, pltpu.HBM)
    fishers = pltpu.with_memory_space_constraint(fishers, pltpu.HBM)
    held, columns, rows = deltas.shape
    half = columns // 2
    tasks, devices = held * lax.axis_size("task"), lax.axis_size(AXES)
    sums_type = jax.ShapeDtypeStruct((2, half, rows), jnp.float32)
    half_type = jax.ShapeDtypeStruct((half, rows), jnp.float32)
    half_input = pltpu.VMEM((held, half, rows), deltas.dtype)
    received = []
    for skip, size in ((0, EARLY), (EARLY, half - EARLY)):
        part_input = pltpu.VMEM((held, size, rows), deltas.dtype)
        sent = pl.pallas_call(
            functools.partial(send_kernel, skip), out_shape=jax.ShapeDtypeStruct((2, size, rows), jnp.float32),
            in_specs=[hbm()] * 2, out_specs=whole(), compiler_params=SMALL,
            scratch_shapes=[part_input, part_input, pltpu.SemaphoreType.DMA((2,))],
        )(deltas, fishers)
        received.append(lax.ppermute(sent, "task", SWAP))
    own, squares = pl.pallas_call(
        own_kernel, out_shape=(sums_type, jax.ShapeDtypeStruct((held, 8, LANES), jnp.float32)),
        in_specs=[hbm()] * 2, out_specs=(whole(), whole()), compiler_params=SMALL,
        scratch_shapes=[
            pltpu.VMEM((held, columns, rows), deltas.dtype), half_input,
            pltpu.SemaphoreType.DMA((2 * held,)), pltpu.SemaphoreType.DMA((held,)),
        ],
    )(deltas, fishers)
    merged, message = pl.pallas_call(
        merge_kernel, out_shape=(half_type, jax.ShapeDtypeStruct((1, LANES), jnp.float32)),
        in_specs=[whole()] * 4, out_specs=(whole(), whole()), compiler_params=SMALL,
    )(own, *received, squares)
    other = lax.ppermute(merged, "task", SWAP)
    message += lax.ppermute(message, "dp", [(i, i ^ 1) for i in range(lax.axis_size("dp"))])
    messages = lax.all_to_all(
        jnp.broadcast_to(message, (devices // 2, LANES)), AXES, 0, 0, tiled=True, axis_index_groups=groups_by_core(FIRST)
    )
    out = pl.pallas_call(
        functools.partial(scale_kernel, tasks), out_shape=jax.ShapeDtypeStruct((columns, rows), jnp.float32),
        in_specs=[whole()] * 3, out_specs=hbm(), compiler_params=SMALL,
        scratch_shapes=[pltpu.VMEM((columns, rows), jnp.float32), pltpu.SemaphoreType.DMA((2 * PIECES,))],
    )(messages, merged, other)
    return out.T


def solution(mesh):
    placed = P("task", "dp", "mp")
    return jax.shard_map(shards, mesh=mesh, in_specs=(placed, placed), out_specs=P("dp", "mp"), check_vma=False)
```

```python
import functools

import jax
import jax.numpy as jnp
from jax import lax
from jax.experimental import pallas as pl
from jax.experimental.pallas import tpu as pltpu
from jax.sharding import PartitionSpec as P

AXES = ("task", "dp", "mp")
SWAP = [(0, 1), (1, 0)]
EPS = 1e-06
LANES = 128
PARTS = ((0, 96), (96, 96), (192, 96))
PIECES = 3
FIRST = (2, 2, 5)
SMALL = pltpu.CompilerParams(vmem_limit_bytes=16 * 1024 * 1024)


def whole():
    return pl.BlockSpec(memory_space=pltpu.VMEM)


def hbm():
    return pl.BlockSpec(memory_space=pltpu.HBM)


def fetches(d_hbm, f_hbm, d_ref, f_ref, sems, start, at, size):
    pairs = []
    for k in range(d_hbm.shape[0]):
        pairs.append(tuple(
            pltpu.make_async_copy(src.at[k, pl.ds(start, size), :], dst.at[k, pl.ds(at, size), :], sems.at[2 * k + i])
            for i, (src, dst) in enumerate(((d_hbm, d_ref), (f_hbm, f_ref)))
        ))
    return pairs


def add_weighted(pairs, d_ref, f_ref, sums_ref):
    _, rows, _ = sums_ref.shape
    for k, pair in enumerate(pairs):
        for copy in pair:
            copy.wait()
        d = d_ref[k, :rows, :].astype(jnp.float32)
        f = f_ref[k, :rows, :].astype(jnp.float32)
        if k == 0:
            sums_ref[0], sums_ref[1] = f * d, f
        else:
            sums_ref[0] += f * d
            sums_ref[1] += f


def send_kernel(skip, d_hbm, f_hbm, sums_ref, d_ref, f_ref, sems):
    _, rows, _ = sums_ref.shape
    half = d_hbm.shape[1] // 2
    start = pl.multiple_of((1 - lax.axis_index("task")) * half + skip, 32)
    copies = [
        pltpu.make_async_copy(src.at[:, pl.ds(start, rows), :], dst, sems.at[i])
        for i, (src, dst) in enumerate(((d_hbm, d_ref), (f_hbm, f_ref)))
    ]
    for copy in copies:
        copy.start()
    for copy in copies:
        copy.wait()

    @pl.loop(0, rows // 32)
    def _(i):
        at = pl.ds(pl.multiple_of(i * 32, 32), 32)
        d = d_ref[:, at, :].astype(jnp.float32)
        f = f_ref[:, at, :].astype(jnp.float32)
        sums_ref[0, at, :] = jnp.sum(f * d, axis=0)
        sums_ref[1, at, :] = jnp.sum(f, axis=0)


def own_kernel(d_hbm, f_hbm, sums_ref, squares_ref, d_ref, f_ref, sems, rest_sems):
    _, rows, _ = sums_ref.shape
    held, both, columns = d_hbm.shape
    task = lax.axis_index("task")
    pairs = fetches(d_hbm, f_hbm, d_ref, f_ref, sems, pl.multiple_of(task * rows, 32), 0, rows)
    for pair in pairs:
        for copy in pair:
            copy.start()
    start = pl.multiple_of((1 - task) * rows, 32)
    rest = [
        pltpu.make_async_copy(
            d_hbm.at[k, pl.ds(start, rows), :], d_ref.at[k, pl.ds(rows, rows), :], rest_sems.at[k]
        )
        for k in range(held)
    ]
    for copy in rest:
        copy.start()
    add_weighted(pairs, d_ref, f_ref, sums_ref)
    for k in range(held):
        rest[k].wait()
        d = d_ref[k].astype(jnp.float32)
        part = jnp.sum((d * d).reshape(both // 8, 8, columns), axis=0)
        squares_ref[k] = part[:, :LANES] + part[:, LANES:]


def merge_kernel(own_ref, *refs):
    *got_refs, squares_ref, merged_ref, message_ref = refs
    columns = own_ref.shape[2]
    at, part = 0, 0.0
    for got_ref in got_refs:
        rows = got_ref.shape[1]
        own = own_ref[:, at : at + rows, :]
        merged = (own[0] + got_ref[0]) / (own[1] + got_ref[1])
        merged_ref[at : at + rows, :] = merged
        part += jnp.sum((merged * merged).reshape(rows // 8, 8, columns), axis=0)
        at += rows
    merged_sum = jnp.sum(part, keepdims=True)
    held = squares_ref.shape[0]
    lane = lax.broadcasted_iota(jnp.int32, (1, LANES), 1)
    first = lax.axis_index("task") * held
    message = jnp.where(lane == 2 * held, merged_sum, 0.0)
    for k in range(held):
        message = jnp.where(lane == first + k, jnp.sum(squares_ref[k], keepdims=True), message)
    message_ref[...] = message


def scale_kernel(tasks, messages_ref, merged_ref, other_ref, out_hbm, scaled_ref, sems):
    rows, _ = merged_ref.shape
    sums = jnp.sum(messages_ref[...], axis=0, keepdims=True)
    lane = lax.broadcasted_iota(jnp.int32, sums.shape, 1)
    target = jnp.sum(jnp.where(lane < tasks, jnp.sqrt(sums + EPS), 0.0), keepdims=True) / tasks
    merged_sq = jnp.sum(jnp.where(lane == tasks, sums, 0.0), keepdims=True)
    rescale = target / jnp.sqrt(merged_sq + EPS)
    task = lax.axis_index("task")
    size = rows // PIECES
    copies = []
    for i, (half_ref, side) in enumerate(((merged_ref, task), (other_ref, 1 - task))):
        for j in range(PIECES):
            at = (i * PIECES + j) * size
            scaled_ref[at : at + size, :] = rescale * half_ref[j * size : (j + 1) * size, :]
            to = pl.multiple_of(side * rows + j * size, 8)
            copies.append(pltpu.make_async_copy(
                scaled_ref.at[at : at + size, :], out_hbm.at[pl.ds(to, size), :], sems.at[i * PIECES + j]
            ))
            copies[-1].start()
    for copy in copies:
        copy.wait()


def groups_by_core(root):
    groups = []
    for core in range(2):
        places = []
        for task in range(2):
            for z in range(8):
                for x_hi in range(2):
                    for y in range(4):
                        place = (2 * x_hi + task, y, z)
                        index = ((task * 8 + z) * 2 + core) * 8 + x_hi * 4 + y
                        places.append((place != root, index))
        groups.append([index for _, index in sorted(places)])
    return groups


def shards(deltas, fishers):
    deltas, fishers = jnp.swapaxes(deltas, 1, 2), jnp.swapaxes(fishers, 1, 2)
    deltas = pltpu.with_memory_space_constraint(deltas, pltpu.HBM)
    fishers = pltpu.with_memory_space_constraint(fishers, pltpu.HBM)
    held, columns, rows = deltas.shape
    half = columns // 2
    tasks, devices = held * lax.axis_size("task"), lax.axis_size(AXES)
    sums_type = jax.ShapeDtypeStruct((2, half, rows), jnp.float32)
    half_type = jax.ShapeDtypeStruct((half, rows), jnp.float32)
    half_input = pltpu.VMEM((held, half, rows), deltas.dtype)
    received = []
    for skip, size in PARTS:
        part_input = pltpu.VMEM((held, size, rows), deltas.dtype)
        sent = pl.pallas_call(
            functools.partial(send_kernel, skip), out_shape=jax.ShapeDtypeStruct((2, size, rows), jnp.float32),
            in_specs=[hbm()] * 2, out_specs=whole(), compiler_params=SMALL,
            scratch_shapes=[part_input, part_input, pltpu.SemaphoreType.DMA((2,))],
        )(deltas, fishers)
        received.append(lax.ppermute(sent, "task", SWAP))
    own, squares = pl.pallas_call(
        own_kernel, out_shape=(sums_type, jax.ShapeDtypeStruct((held, 8, LANES), jnp.float32)),
        in_specs=[hbm()] * 2, out_specs=(whole(), whole()), compiler_params=SMALL,
        scratch_shapes=[
            pltpu.VMEM((held, columns, rows), deltas.dtype), half_input,
            pltpu.SemaphoreType.DMA((2 * held,)), pltpu.SemaphoreType.DMA((held,)),
        ],
    )(deltas, fishers)
    merged, message = pl.pallas_call(
        merge_kernel, out_shape=(half_type, jax.ShapeDtypeStruct((1, LANES), jnp.float32)),
        in_specs=[whole()] * (2 + len(PARTS)), out_specs=(whole(), whole()), compiler_params=SMALL,
    )(own, *received, squares)
    other = lax.ppermute(merged, "task", SWAP)
    message += lax.ppermute(message, "dp", [(i, i ^ 1) for i in range(lax.axis_size("dp"))])
    messages = lax.all_to_all(
        jnp.broadcast_to(message, (devices // 2, LANES)), AXES, 0, 0, tiled=True, axis_index_groups=groups_by_core(FIRST)
    )
    out = pl.pallas_call(
        functools.partial(scale_kernel, tasks), out_shape=jax.ShapeDtypeStruct((columns, rows), jnp.float32),
        in_specs=[whole()] * 3, out_specs=hbm(), compiler_params=SMALL,
        scratch_shapes=[pltpu.VMEM((columns, rows), jnp.float32), pltpu.SemaphoreType.DMA((2 * PIECES,))],
    )(messages, merged, other)
    return out.T


def solution(mesh):
    placed = P("task", "dp", "mp")
    return jax.shard_map(shards, mesh=mesh, in_specs=(placed, placed), out_specs=P("dp", "mp"), check_vma=False)
```

```python
import functools

import jax
import jax.numpy as jnp
from jax import lax
from jax.experimental import pallas as pl
from jax.experimental.pallas import tpu as pltpu
from jax.sharding import PartitionSpec as P

AXES = ("task", "dp", "mp")
SWAP = [(0, 1), (1, 0)]
EPS = 1e-06
LANES = 128
PARTS = ((0, 64), (64, 160), (224, 64))
PIECES = 3
FIRST = (2, 2, 5)
SMALL = pltpu.CompilerParams(vmem_limit_bytes=16 * 1024 * 1024)


def whole():
    return pl.BlockSpec(memory_space=pltpu.VMEM)


def hbm():
    return pl.BlockSpec(memory_space=pltpu.HBM)


def fetches(d_hbm, f_hbm, d_ref, f_ref, sems, start, at, size):
    pairs = []
    for k in range(d_hbm.shape[0]):
        pairs.append(tuple(
            pltpu.make_async_copy(src.at[k, pl.ds(start, size), :], dst.at[k, pl.ds(at, size), :], sems.at[2 * k + i])
            for i, (src, dst) in enumerate(((d_hbm, d_ref), (f_hbm, f_ref)))
        ))
    return pairs


def add_weighted(pairs, d_ref, f_ref, sums_ref):
    _, rows, _ = sums_ref.shape
    for k, pair in enumerate(pairs):
        for copy in pair:
            copy.wait()
        d = d_ref[k, :rows, :].astype(jnp.float32)
        f = f_ref[k, :rows, :].astype(jnp.float32)
        if k == 0:
            sums_ref[0], sums_ref[1] = f * d, f
        else:
            sums_ref[0] += f * d
            sums_ref[1] += f


def send_kernel(skip, d_hbm, f_hbm, sums_ref, d_ref, f_ref, sems):
    _, rows, _ = sums_ref.shape
    half = d_hbm.shape[1] // 2
    start = pl.multiple_of((1 - lax.axis_index("task")) * half + skip, 32)
    copies = [
        pltpu.make_async_copy(src.at[:, pl.ds(start, rows), :], dst, sems.at[i])
        for i, (src, dst) in enumerate(((d_hbm, d_ref), (f_hbm, f_ref)))
    ]
    for copy in copies:
        copy.start()
    for copy in copies:
        copy.wait()

    @pl.loop(0, rows // 32)
    def _(i):
        at = pl.ds(pl.multiple_of(i * 32, 32), 32)
        d = d_ref[:, at, :].astype(jnp.float32)
        f = f_ref[:, at, :].astype(jnp.float32)
        sums_ref[0, at, :] = jnp.sum(f * d, axis=0)
        sums_ref[1, at, :] = jnp.sum(f, axis=0)


def own_kernel(d_hbm, f_hbm, sums_ref, squares_ref, d_ref, f_ref, sems, rest_sems):
    _, rows, _ = sums_ref.shape
    held, both, columns = d_hbm.shape
    task = lax.axis_index("task")
    pairs = fetches(d_hbm, f_hbm, d_ref, f_ref, sems, pl.multiple_of(task * rows, 32), 0, rows)
    for pair in pairs:
        for copy in pair:
            copy.start()
    start = pl.multiple_of((1 - task) * rows, 32)
    rest = [
        pltpu.make_async_copy(
            d_hbm.at[k, pl.ds(start, rows), :], d_ref.at[k, pl.ds(rows, rows), :], rest_sems.at[k]
        )
        for k in range(held)
    ]
    for copy in rest:
        copy.start()
    add_weighted(pairs, d_ref, f_ref, sums_ref)
    for k in range(held):
        rest[k].wait()
        d = d_ref[k].astype(jnp.float32)
        part = jnp.sum((d * d).reshape(both // 8, 8, columns), axis=0)
        squares_ref[k] = part[:, :LANES] + part[:, LANES:]


def early_kernel(own_ref, *refs):
    *got_refs, merged_ref, part_ref = refs
    columns = own_ref.shape[2]
    at, part = 0, 0.0
    for got_ref in got_refs:
        rows = got_ref.shape[1]
        own = own_ref[:, at : at + rows, :]
        merged = (own[0] + got_ref[0]) / (own[1] + got_ref[1])
        merged_ref[at : at + rows, :] = merged
        part += jnp.sum((merged * merged).reshape(rows // 8, 8, columns), axis=0)
        at += rows
    part_ref[...] = part


def merge_kernel(own_ref, got_ref, early_ref, part_ref, squares_ref, merged_ref, message_ref):
    columns = own_ref.shape[2]
    rows, at = got_ref.shape[1], early_ref.shape[0]
    own = own_ref[:, at : at + rows, :]
    merged = (own[0] + got_ref[0]) / (own[1] + got_ref[1])
    merged_ref[:at, :] = early_ref[...]
    merged_ref[at : at + rows, :] = merged
    part = part_ref[...] + jnp.sum((merged * merged).reshape(rows // 8, 8, columns), axis=0)
    merged_sum = jnp.sum(part, keepdims=True)
    held = squares_ref.shape[0]
    lane = lax.broadcasted_iota(jnp.int32, (1, LANES), 1)
    first = lax.axis_index("task") * held
    message = jnp.where(lane == 2 * held, merged_sum, 0.0)
    for k in range(held):
        message = jnp.where(lane == first + k, jnp.sum(squares_ref[k], keepdims=True), message)
    message_ref[...] = message


def scale_kernel(tasks, messages_ref, merged_ref, other_ref, out_hbm, scaled_ref, sems):
    rows, _ = merged_ref.shape
    sums = jnp.sum(messages_ref[...], axis=0, keepdims=True)
    lane = lax.broadcasted_iota(jnp.int32, sums.shape, 1)
    target = jnp.sum(jnp.where(lane < tasks, jnp.sqrt(sums + EPS), 0.0), keepdims=True) / tasks
    merged_sq = jnp.sum(jnp.where(lane == tasks, sums, 0.0), keepdims=True)
    rescale = target / jnp.sqrt(merged_sq + EPS)
    task = lax.axis_index("task")
    size = rows // PIECES
    copies = []
    for i, (half_ref, side) in enumerate(((merged_ref, task), (other_ref, 1 - task))):
        for j in range(PIECES):
            at = (i * PIECES + j) * size
            scaled_ref[at : at + size, :] = rescale * half_ref[j * size : (j + 1) * size, :]
            to = pl.multiple_of(side * rows + j * size, 8)
            copies.append(pltpu.make_async_copy(
                scaled_ref.at[at : at + size, :], out_hbm.at[pl.ds(to, size), :], sems.at[i * PIECES + j]
            ))
            copies[-1].start()
    for copy in copies:
        copy.wait()


def groups_by_core(root):
    groups = []
    for core in range(2):
        places = []
        for task in range(2):
            for z in range(8):
                for x_hi in range(2):
                    for y in range(4):
                        place = (2 * x_hi + task, y, z)
                        index = ((task * 8 + z) * 2 + core) * 8 + x_hi * 4 + y
                        places.append((place != root, index))
        groups.append([index for _, index in sorted(places)])
    return groups


def shards(deltas, fishers):
    deltas, fishers = jnp.swapaxes(deltas, 1, 2), jnp.swapaxes(fishers, 1, 2)
    deltas = pltpu.with_memory_space_constraint(deltas, pltpu.HBM)
    fishers = pltpu.with_memory_space_constraint(fishers, pltpu.HBM)
    held, columns, rows = deltas.shape
    half = columns // 2
    tasks, devices = held * lax.axis_size("task"), lax.axis_size(AXES)
    sums_type = jax.ShapeDtypeStruct((2, half, rows), jnp.float32)
    half_type = jax.ShapeDtypeStruct((half, rows), jnp.float32)
    half_input = pltpu.VMEM((held, half, rows), deltas.dtype)
    received = []
    for skip, size in PARTS:
        part_input = pltpu.VMEM((held, size, rows), deltas.dtype)
        sent = pl.pallas_call(
            functools.partial(send_kernel, skip), out_shape=jax.ShapeDtypeStruct((2, size, rows), jnp.float32),
            in_specs=[hbm()] * 2, out_specs=whole(), compiler_params=SMALL,
            scratch_shapes=[part_input, part_input, pltpu.SemaphoreType.DMA((2,))],
        )(deltas, fishers)
        received.append(lax.ppermute(sent, "task", SWAP))
    own, squares = pl.pallas_call(
        own_kernel, out_shape=(sums_type, jax.ShapeDtypeStruct((held, 8, LANES), jnp.float32)),
        in_specs=[hbm()] * 2, out_specs=(whole(), whole()), compiler_params=SMALL,
        scratch_shapes=[
            pltpu.VMEM((held, columns, rows), deltas.dtype), half_input,
            pltpu.SemaphoreType.DMA((2 * held,)), pltpu.SemaphoreType.DMA((held,)),
        ],
    )(deltas, fishers)
    *early_got, last = received
    done = half - PARTS[-1][1]
    early, part = pl.pallas_call(
        early_kernel,
        out_shape=(jax.ShapeDtypeStruct((done, rows), jnp.float32), jax.ShapeDtypeStruct((8, rows), jnp.float32)),
        in_specs=[whole()] * len(PARTS), out_specs=(whole(), whole()), compiler_params=SMALL,
    )(own, *early_got)
    merged, message = pl.pallas_call(
        merge_kernel, out_shape=(half_type, jax.ShapeDtypeStruct((1, LANES), jnp.float32)),
        in_specs=[whole()] * 5, out_specs=(whole(), whole()), compiler_params=SMALL,
    )(own, last, early, part, squares)
    other = lax.ppermute(merged, "task", SWAP)
    message += lax.ppermute(message, "dp", [(i, i ^ 1) for i in range(lax.axis_size("dp"))])
    messages = lax.all_to_all(
        jnp.broadcast_to(message, (devices // 2, LANES)), AXES, 0, 0, tiled=True, axis_index_groups=groups_by_core(FIRST)
    )
    out = pl.pallas_call(
        functools.partial(scale_kernel, tasks), out_shape=jax.ShapeDtypeStruct((columns, rows), jnp.float32),
        in_specs=[whole()] * 3, out_specs=hbm(), compiler_params=SMALL,
        scratch_shapes=[pltpu.VMEM((columns, rows), jnp.float32), pltpu.SemaphoreType.DMA((2 * PIECES,))],
    )(messages, merged, other)
    return out.T


def solution(mesh):
    placed = P("task", "dp", "mp")
    return jax.shard_map(shards, mesh=mesh, in_specs=(placed, placed), out_specs=P("dp", "mp"), check_vma=False)
```

```python
import functools

import jax
import jax.numpy as jnp
from jax import lax
from jax.experimental import pallas as pl
from jax.experimental.pallas import tpu as pltpu
from jax.sharding import PartitionSpec as P

AXES = ("task", "dp", "mp")
SWAP = [(0, 1), (1, 0)]
EPS = 1e-06
LANES = 128
PARTS = ((0, 96), (96, 160), (256, 32))
PIECES = 3
FIRST = (2, 2, 5)
SMALL = pltpu.CompilerParams(vmem_limit_bytes=16 * 1024 * 1024)


def whole():
    return pl.BlockSpec(memory_space=pltpu.VMEM)


def hbm():
    return pl.BlockSpec(memory_space=pltpu.HBM)


def fetches(d_hbm, f_hbm, d_ref, f_ref, sems, start, at, size):
    pairs = []
    for k in range(d_hbm.shape[0]):
        pairs.append(tuple(
            pltpu.make_async_copy(src.at[k, pl.ds(start, size), :], dst.at[k, pl.ds(at, size), :], sems.at[2 * k + i])
            for i, (src, dst) in enumerate(((d_hbm, d_ref), (f_hbm, f_ref)))
        ))
    return pairs


def add_weighted(pairs, d_ref, f_ref, sums_ref):
    _, rows, _ = sums_ref.shape
    for k, pair in enumerate(pairs):
        for copy in pair:
            copy.wait()
        d = d_ref[k, :rows, :].astype(jnp.float32)
        f = f_ref[k, :rows, :].astype(jnp.float32)
        if k == 0:
            sums_ref[0], sums_ref[1] = f * d, f
        else:
            sums_ref[0] += f * d
            sums_ref[1] += f


def send_kernel(skip, d_hbm, f_hbm, sums_ref, d_ref, f_ref, sems):
    _, rows, _ = sums_ref.shape
    half = d_hbm.shape[1] // 2
    start = pl.multiple_of((1 - lax.axis_index("task")) * half + skip, 32)
    copies = [
        pltpu.make_async_copy(src.at[:, pl.ds(start, rows), :], dst, sems.at[i])
        for i, (src, dst) in enumerate(((d_hbm, d_ref), (f_hbm, f_ref)))
    ]
    for copy in copies:
        copy.start()
    for copy in copies:
        copy.wait()

    @pl.loop(0, rows // 32)
    def _(i):
        at = pl.ds(pl.multiple_of(i * 32, 32), 32)
        d = d_ref[:, at, :].astype(jnp.float32)
        f = f_ref[:, at, :].astype(jnp.float32)
        sums_ref[0, at, :] = jnp.sum(f * d, axis=0)
        sums_ref[1, at, :] = jnp.sum(f, axis=0)


def own_kernel(d_hbm, f_hbm, sums_ref, squares_ref, d_ref, f_ref, sems, rest_sems):
    _, rows, _ = sums_ref.shape
    held, both, columns = d_hbm.shape
    task = lax.axis_index("task")
    pairs = fetches(d_hbm, f_hbm, d_ref, f_ref, sems, pl.multiple_of(task * rows, 32), 0, rows)
    for pair in pairs:
        for copy in pair:
            copy.start()
    start = pl.multiple_of((1 - task) * rows, 32)
    rest = [
        pltpu.make_async_copy(
            d_hbm.at[k, pl.ds(start, rows), :], d_ref.at[k, pl.ds(rows, rows), :], rest_sems.at[k]
        )
        for k in range(held)
    ]
    for copy in rest:
        copy.start()
    add_weighted(pairs, d_ref, f_ref, sums_ref)
    for k in range(held):
        rest[k].wait()
        d = d_ref[k].astype(jnp.float32)
        part = jnp.sum((d * d).reshape(both // 8, 8, columns), axis=0)
        squares_ref[k] = part[:, :LANES] + part[:, LANES:]


def early_kernel(own_ref, *refs):
    *got_refs, merged_ref, part_ref = refs
    columns = own_ref.shape[2]
    at, part = 0, 0.0
    for got_ref in got_refs:
        rows = got_ref.shape[1]
        own = own_ref[:, at : at + rows, :]
        merged = (own[0] + got_ref[0]) / (own[1] + got_ref[1])
        merged_ref[at : at + rows, :] = merged
        part += jnp.sum((merged * merged).reshape(rows // 8, 8, columns), axis=0)
        at += rows
    part_ref[...] = part


def merge_kernel(own_ref, got_ref, early_ref, part_ref, squares_ref, merged_ref, message_ref):
    columns = own_ref.shape[2]
    rows, at = got_ref.shape[1], early_ref.shape[0]
    own = own_ref[:, at : at + rows, :]
    merged = (own[0] + got_ref[0]) / (own[1] + got_ref[1])
    merged_ref[:at, :] = early_ref[...]
    merged_ref[at : at + rows, :] = merged
    part = part_ref[...] + jnp.sum((merged * merged).reshape(rows // 8, 8, columns), axis=0)
    merged_sum = jnp.sum(part, keepdims=True)
    held = squares_ref.shape[0]
    lane = lax.broadcasted_iota(jnp.int32, (1, LANES), 1)
    first = lax.axis_index("task") * held
    message = jnp.where(lane == 2 * held, merged_sum, 0.0)
    for k in range(held):
        message = jnp.where(lane == first + k, jnp.sum(squares_ref[k], keepdims=True), message)
    message_ref[...] = message


def scale_kernel(tasks, messages_ref, merged_ref, other_ref, out_hbm, scaled_ref, sems):
    rows, _ = merged_ref.shape
    sums = jnp.sum(messages_ref[...], axis=0, keepdims=True)
    lane = lax.broadcasted_iota(jnp.int32, sums.shape, 1)
    target = jnp.sum(jnp.where(lane < tasks, jnp.sqrt(sums + EPS), 0.0), keepdims=True) / tasks
    merged_sq = jnp.sum(jnp.where(lane == tasks, sums, 0.0), keepdims=True)
    rescale = target / jnp.sqrt(merged_sq + EPS)
    task = lax.axis_index("task")
    size = rows // PIECES
    copies = []
    for i, (half_ref, side) in enumerate(((merged_ref, task), (other_ref, 1 - task))):
        for j in range(PIECES):
            at = (i * PIECES + j) * size
            scaled_ref[at : at + size, :] = rescale * half_ref[j * size : (j + 1) * size, :]
            to = pl.multiple_of(side * rows + j * size, 8)
            copies.append(pltpu.make_async_copy(
                scaled_ref.at[at : at + size, :], out_hbm.at[pl.ds(to, size), :], sems.at[i * PIECES + j]
            ))
            copies[-1].start()
    for copy in copies:
        copy.wait()


def groups_by_core(root):
    groups = []
    for core in range(2):
        places = []
        for task in range(2):
            for z in range(8):
                for x_hi in range(2):
                    for y in range(4):
                        place = (2 * x_hi + task, y, z)
                        index = ((task * 8 + z) * 2 + core) * 8 + x_hi * 4 + y
                        places.append((place != root, index))
        groups.append([index for _, index in sorted(places)])
    return groups


def shards(deltas, fishers):
    deltas, fishers = jnp.swapaxes(deltas, 1, 2), jnp.swapaxes(fishers, 1, 2)
    deltas = pltpu.with_memory_space_constraint(deltas, pltpu.HBM)
    fishers = pltpu.with_memory_space_constraint(fishers, pltpu.HBM)
    held, columns, rows = deltas.shape
    half = columns // 2
    tasks, devices = held * lax.axis_size("task"), lax.axis_size(AXES)
    sums_type = jax.ShapeDtypeStruct((2, half, rows), jnp.float32)
    half_type = jax.ShapeDtypeStruct((half, rows), jnp.float32)
    half_input = pltpu.VMEM((held, half, rows), deltas.dtype)
    received = []
    for skip, size in PARTS:
        part_input = pltpu.VMEM((held, size, rows), deltas.dtype)
        sent = pl.pallas_call(
            functools.partial(send_kernel, skip), out_shape=jax.ShapeDtypeStruct((2, size, rows), jnp.float32),
            in_specs=[hbm()] * 2, out_specs=whole(), compiler_params=SMALL,
            scratch_shapes=[part_input, part_input, pltpu.SemaphoreType.DMA((2,))],
        )(deltas, fishers)
        received.append(lax.ppermute(sent, "task", SWAP))
    own, squares = pl.pallas_call(
        own_kernel, out_shape=(sums_type, jax.ShapeDtypeStruct((held, 8, LANES), jnp.float32)),
        in_specs=[hbm()] * 2, out_specs=(whole(), whole()), compiler_params=SMALL,
        scratch_shapes=[
            pltpu.VMEM((held, columns, rows), deltas.dtype), half_input,
            pltpu.SemaphoreType.DMA((2 * held,)), pltpu.SemaphoreType.DMA((held,)),
        ],
    )(deltas, fishers)
    *early_got, last = received
    done = half - PARTS[-1][1]
    early, part = pl.pallas_call(
        early_kernel,
        out_shape=(jax.ShapeDtypeStruct((done, rows), jnp.float32), jax.ShapeDtypeStruct((8, rows), jnp.float32)),
        in_specs=[whole()] * len(PARTS), out_specs=(whole(), whole()), compiler_params=SMALL,
    )(own, *early_got)
    merged, message = pl.pallas_call(
        merge_kernel, out_shape=(half_type, jax.ShapeDtypeStruct((1, LANES), jnp.float32)),
        in_specs=[whole()] * 5, out_specs=(whole(), whole()), compiler_params=SMALL,
    )(own, last, early, part, squares)
    other = lax.ppermute(merged, "task", SWAP)
    message += lax.ppermute(message, "dp", [(i, i ^ 1) for i in range(lax.axis_size("dp"))])
    messages = lax.all_to_all(
        jnp.broadcast_to(message, (devices // 2, LANES)), AXES, 0, 0, tiled=True, axis_index_groups=groups_by_core(FIRST)
    )
    out = pl.pallas_call(
        functools.partial(scale_kernel, tasks), out_shape=jax.ShapeDtypeStruct((columns, rows), jnp.float32),
        in_specs=[whole()] * 3, out_specs=hbm(), compiler_params=SMALL,
        scratch_shapes=[pltpu.VMEM((columns, rows), jnp.float32), pltpu.SemaphoreType.DMA((2 * PIECES,))],
    )(messages, merged, other)
    return out.T


def solution(mesh):
    placed = P("task", "dp", "mp")
    return jax.shard_map(shards, mesh=mesh, in_specs=(placed, placed), out_specs=P("dp", "mp"), check_vma=False)
```
